32 devices in a mesh: parts: 2 (over y), aper: 4 (over z), rng: 2 (over x), sub: 2 (over core).
Axes of the slice: x: 2, y: 2, z: 4, core: 2. Of those that a mesh axis runs over, the one named last changes fastest.
Arguments:
- echoes: bfloat16 [2, 1024, 2048], P(None, ('parts', 'aper', 'sub'), 'rng'), parts along dimension 1, may hold values from -6 to 6
- chirp: bfloat16 [2, 512], replicated, may hold values from -0.1875 to 0.1875
- pulse_phase: float32 [1024, 64], P(('parts', 'aper', 'sub')), parts along dimension 0, may hold values from -3.140625 to 3.140625
- pulse_shift: int32 [1024, 64], P(('parts', 'aper', 'sub')), parts along dimension 0, may hold values from -8 to 8
- kernel_taps: int32 [2, 2, 8, 512], P(None, None, None, ('parts', 'aper', 'sub')), parts along dimension 3, may hold values from 0 to 31
- merge_shift: int32 [2, 2, 512], P(None, None, ('parts', 'aper', 'sub')), parts along dimension 2, may hold values from -8 to 8
- kernel_weights: float32 [2, 2, 2, 8, 512], P(None, None, None, None, ('parts', 'aper', 'sub')), parts along dimension 4, may hold values from -1 to 1
Outputs:
- image: bfloat16 [2, 512, 2048], P(None, ('parts', 'aper', 'sub'), 'rng'), parts along dimension 1
The draws below stay inside these ranges and needn't reach their ends.
There are 2 independent parts, one for each index of `parts`. The reference program is written for one: setup_inputs(seed, part) draws one part's arguments, and reference() takes and returns one part's arrays. A program takes and returns all parts, laid end to end along the dimension named above; an argument that names none is the same for every part. Nothing has to cross between parts.
All inputs are finite; a program needn't handle non-finite values.
Results may differ from the reference program's by a relative error of at most 0.0099.
Values may be sent and summed in bfloat16 or wider, within the bound.
A program may use at most 128 MiB of HBM per device.

```python
import math
import jax
import jax.numpy as jnp
import numpy as np
from jax import lax

BINS = 2048
TAPS = 512
REACH = 8
KERNEL = 8
BEAM_DEV = 32
PULSE_SUB = 128
LEVELS = 2
BEAM_BASE = 64
BEAM_ROWS = 256
PULSES = 512
N_APER = 4


def with_ends(result, own_key, low, top_value):
    place = [jax.random.randint(jax.random.fold_in(own_key, axis), (), 0, length) for axis, length in enumerate(result.shape)]
    longest = result.shape.index(max(result.shape))
    neighbour = place[:longest] + [(place[longest] + 1) % result.shape[longest]] + place[longest + 1:]
    return result.at[tuple(place)].set(low).at[tuple(neighbour)].set(top_value)


def block_scale(key, extent, split, low, largest):
    loudness = 1.0
    for axis_at, blocks in split:
        draws = jax.random.uniform(jax.random.fold_in(jax.random.fold_in(key, 6), axis_at), (blocks,), jnp.float32, low / len(split), largest / len(split))
        loudness = loudness * jnp.repeat(jnp.exp(draws), extent[axis_at] // blocks).reshape((-1,) + (1,) * (len(extent) - 1 - axis_at))
    return loudness


def noise(rng, dims, width, reach, cuts=(), kind=jnp.bfloat16):
    factor_of = block_scale(rng, dims, cuts, -0.22, 0.18) if cuts else 1.0
    array = jax.random.normal(rng, dims, jnp.float32) * width * factor_of
    return jnp.minimum(jnp.maximum(array, -reach), reach).astype(kind)


def setup_inputs(seed: int = 0, part: int = 0) -> dict:
    streams_of = jax.random.split(jax.random.key(seed), 8)
    part_splits = jax.random.split(jax.random.fold_in(streams_of[7], part), 8)
    return {
        "echoes": noise(part_splits[0], (2, PULSES, BINS), 1.0, 6.0, ((1, 8), (2, 2))),
        "chirp": noise(streams_of[1], (2, TAPS), (2 * TAPS) ** -0.5, 0.1875),
        "pulse_phase": jnp.clip(jax.random.uniform(part_splits[2], (PULSES, BEAM_BASE), jnp.float32, -3.140625, 3.140625), -3.140625, 3.140625),
        "pulse_shift": with_ends(jax.random.randint(part_splits[3], (PULSES, BEAM_BASE), -REACH, REACH + 1), jax.random.fold_in(part_splits[3], 1), -REACH, REACH).astype(jnp.int32),
        "kernel_taps": with_ends(jax.random.randint(part_splits[4], (LEVELS, 2, KERNEL, BEAM_ROWS), 0, BEAM_DEV), jax.random.fold_in(part_splits[4], 1), 0, BEAM_DEV - 1).astype(jnp.int32),
        "merge_shift": with_ends(jax.random.randint(part_splits[5], (LEVELS, 2, BEAM_ROWS), -REACH, REACH + 1), jax.random.fold_in(part_splits[5], 1), -REACH, REACH).astype(jnp.int32),
        "kernel_weights": noise(part_splits[6], (2, LEVELS, 2, KERNEL, BEAM_ROWS), (4 * KERNEL) ** -0.5, 1.0, ((4, 8),), jnp.float32),
    }


def compress(echoes, chirp):
    row_ids = jnp.arange(BINS, dtype=jnp.int32)[:, None]
    col_ids = jnp.arange(BINS, dtype=jnp.int32)[None, :]
    lag_bins = row_ids - col_ids
    inside = (lag_bins >= 0) & (lag_bins < TAPS)
    tap_index = jnp.clip(lag_bins, 0, TAPS - 1)
    real_tap = jnp.where(inside, chirp[0][tap_index], jnp.zeros((), chirp.dtype))
    imag_tap = jnp.where(inside, chirp[1][tap_index], jnp.zeros((), chirp.dtype))
    real_out = jnp.dot(echoes[0], real_tap, preferred_element_type=jnp.float32) + jnp.dot(echoes[1], imag_tap, preferred_element_type=jnp.float32)
    imag_out = jnp.dot(echoes[1], real_tap, preferred_element_type=jnp.float32) - jnp.dot(echoes[0], imag_tap, preferred_element_type=jnp.float32)
    return jnp.stack([real_out, imag_out]).astype(jnp.bfloat16)

def backproject(compressed, pulse_phase, pulse_shift):
    scale = 1.0 / math.sqrt(PULSE_SUB)
    real_w = (jnp.cos(pulse_phase) * scale).astype(jnp.bfloat16)
    imag_w = (jnp.sin(pulse_phase) * scale).astype(jnp.bfloat16)
    padded = jnp.pad(compressed, ((0, 0), (0, 0), (REACH, REACH)))

    def one_block(block):
        start = (block * PULSE_SUB).astype(jnp.int32)
        data_block = lax.dynamic_slice_in_dim(padded, start, PULSE_SUB, 1)
        real_block = lax.dynamic_slice_in_dim(real_w, start, PULSE_SUB, 0)
        imag_block = lax.dynamic_slice_in_dim(imag_w, start, PULSE_SUB, 0)
        shift_block = lax.dynamic_slice_in_dim(pulse_shift, start, PULSE_SUB, 0)
        zero_value = jnp.zeros((), real_block.dtype)
        summed_re = jnp.zeros((BEAM_BASE, BINS), jnp.float32)
        summed_im = jnp.zeros((BEAM_BASE, BINS), jnp.float32)
        for offset in range(-REACH, REACH + 1):
            matches = shift_block == offset
            real_q = jnp.where(matches, real_block, zero_value).T
            imag_q = jnp.where(matches, imag_block, zero_value).T
            window = data_block[:, :, REACH + offset:REACH + offset + BINS]
            summed_re = summed_re + jnp.dot(real_q, window[0], preferred_element_type=jnp.float32) - jnp.dot(imag_q, window[1], preferred_element_type=jnp.float32)
            summed_im = summed_im + jnp.dot(real_q, window[1], preferred_element_type=jnp.float32) + jnp.dot(imag_q, window[0], preferred_element_type=jnp.float32)
        return jnp.stack([summed_re, summed_im]).astype(jnp.bfloat16)
    blocks = lax.map(one_block, jnp.arange(N_APER, dtype=jnp.int32))
    return blocks.transpose(1, 0, 2, 3).reshape(2, BEAM_ROWS, BINS)

def merge_level(image, level, kernel_taps, merge_shift, kernel_weights):
    block_count = BEAM_ROWS // BEAM_DEV
    child_blocks = BEAM_BASE * 2 ** level // BEAM_DEV
    block_ids = np.arange(block_count)
    base_ids = block_ids - child_blocks * (block_ids // child_blocks % 2)
    blocks = image.reshape(2, block_count, BEAM_DEV, BINS)
    beam_ids = jnp.arange(BEAM_DEV, dtype=jnp.int32)
    summed_re = jnp.zeros((block_count, BEAM_DEV, BINS), jnp.float32)
    summed_im = jnp.zeros((block_count, BEAM_DEV, BINS), jnp.float32)
    for child_index in range(2):
        source = blocks[:, base_ids + child_index * child_blocks].astype(jnp.float32)
        source = jnp.pad(source, ((0, 0), (0, 0), (0, 0), (REACH, REACH)))
        matches = kernel_taps[level, child_index][:, :, None] == beam_ids[None, None, :]
        real_k = lax.optimization_barrier(jnp.sum(jnp.where(matches, kernel_weights[0, level, child_index][:, :, None], 0.0), axis=0)).astype(jnp.bfloat16)
        imag_k = lax.optimization_barrier(jnp.sum(jnp.where(matches, kernel_weights[1, level, child_index][:, :, None], 0.0), axis=0)).astype(jnp.bfloat16)
        shifts = merge_shift[level, child_index][:, None]
        zero_value = jnp.zeros((), real_k.dtype)
        for offset in range(-REACH, REACH + 1):
            chosen = shifts == offset
            real_sel = jnp.where(chosen, real_k, zero_value).astype(jnp.float32).reshape(block_count, BEAM_DEV, BEAM_DEV)
            imag_sel = jnp.where(chosen, imag_k, zero_value).astype(jnp.float32).reshape(block_count, BEAM_DEV, BEAM_DEV)
            window = source[..., REACH + offset:REACH + offset + BINS]
            summed_re = summed_re + jnp.einsum('kij,kjr->kir', real_sel, window[0]) - jnp.einsum('kij,kjr->kir', imag_sel, window[1])
            summed_im = summed_im + jnp.einsum('kij,kjr->kir', real_sel, window[1]) + jnp.einsum('kij,kjr->kir', imag_sel, window[0])
    merged = jnp.stack([summed_re, summed_im]).astype(jnp.bfloat16)
    return merged.reshape(2, BEAM_ROWS, BINS)

def reference(echoes, chirp, pulse_phase, pulse_shift, kernel_taps, merge_shift, kernel_weights):
    compressed = compress(echoes, chirp)
    image = backproject(compressed, pulse_phase, pulse_shift)
    for level in range(LEVELS):
        image = merge_level(image, level, kernel_taps, merge_shift, kernel_weights)
    return image
```

```python
import functools
import math

import jax
import jax.numpy as jnp
from jax import lax
from jax.experimental import pallas as pl
from jax.experimental.pallas import tpu as pltpu
from jax.sharding import PartitionSpec as P

REACH = 8
EDGE = 128
TILE = 256
MESH = pl.DeviceIdType.MESH
F32 = jnp.float32
BF16 = jnp.bfloat16


def roll_left(value, by):
    width = value.shape[1]
    by = by % width
    return value if by == 0 else pltpu.roll(value, width - by, 1)


def image_kernel(
    n_rng, n_aper, levels, halos,
    echoes, chirp, phase, shift, ktaps, mshift, kweights,
    out,
    cells, filt, phases, shifts, select, pulses, products, image, sibling, kernels, row_shift,
    own_sem, halo_send, halo_recv, sub_send, sub_recv, lev_send, lev_recv,
):
    rng = lax.axis_index("rng")
    aper = lax.axis_index("aper")
    sub = lax.axis_index("sub")
    local, slab = echoes.shape[1], echoes.shape[2]
    n_taps = chirp.shape[1]
    beams = out.shape[1]
    rows = 2 * beams
    width = slab + 2 * EDGE
    window = TILE + n_taps
    offsets = 2 * REACH + 1
    reach_devs = len(halos)

    barrier = pltpu.get_barrier_semaphore()
    pl.semaphore_signal(barrier, inc=1, device_id={"sub": 1 - sub}, device_id_type=MESH)

    def aper_partner(level):
        stride = 2**level
        side = lax.rem(aper // stride, 2)
        return aper + stride - 2 * stride * side, side

    for level in range(levels):
        pl.semaphore_signal(
            barrier, inc=1, device_id={"aper": aper_partner(level)[0]}, device_id_type=MESH
        )
    for dist in range(1, reach_devs + 1):
        @pl.when(rng + dist < n_rng)
        def _():
            pl.semaphore_signal(barrier, inc=1, device_id={"rng": rng + dist}, device_id_type=MESH)

        @pl.when(rng >= dist)
        def _():
            pl.semaphore_signal(barrier, inc=1, device_id={"rng": rng - dist}, device_id_type=MESH)

    own_copy = pltpu.make_async_copy(echoes, cells.at[:, :, pl.ds(EDGE, slab)], own_sem)
    own_copy.start()
    if reach_devs >= n_rng - 1:
        rng_peers = n_rng - 1
    else:
        rng_peers = jnp.minimum(rng, reach_devs) + jnp.minimum(n_rng - 1 - rng, reach_devs)
    pl.semaphore_wait(barrier, 1 + levels + rng_peers)

    def right_copy(index):
        dist = index + 1
        return pltpu.make_async_remote_copy(
            src_ref=echoes.at[:, :, pl.ds(0, halos[index])],
            dst_ref=cells.at[:, :, pl.ds(EDGE + dist * slab, halos[index])],
            send_sem=halo_send.at[index],
            recv_sem=halo_recv.at[index],
            device_id={"rng": rng - dist},
            device_id_type=MESH,
        )

    left_copy = pltpu.make_async_remote_copy(
        src_ref=echoes.at[:, :, pl.ds(slab - EDGE, EDGE)],
        dst_ref=cells.at[:, :, pl.ds(0, EDGE)],
        send_sem=halo_send.at[reach_devs],
        recv_sem=halo_recv.at[reach_devs],
        device_id={"rng": rng + 1},
        device_id_type=MESH,
    )
    for index in range(reach_devs):
        @pl.when(rng >= index + 1)
        def _():
            right_copy(index).start()

        @pl.when(rng + index + 1 >= n_rng)
        def _():
            cells[:, :, EDGE + (index + 1) * slab : EDGE + (index + 1) * slab + halos[index]] = (
                jnp.zeros((2, local, halos[index]), BF16)
            )

    @pl.when(rng + 1 < n_rng)
    def _():
        left_copy.start()

    @pl.when(rng == 0)
    def _():
        cells[:, :, 0:EDGE] = jnp.zeros((2, local, EDGE), BF16)

    def sub_copy(src, dst, index):
        return pltpu.make_async_remote_copy(
            src_ref=src,
            dst_ref=dst,
            send_sem=sub_send.at[index],
            recv_sem=sub_recv.at[index],
            device_id={"sub": 1 - sub},
            device_id_type=MESH,
        )

    phase_copy = sub_copy(phase, phases, 0)
    shift_copy = sub_copy(shift, shifts, 1)
    phase_copy.start()
    shift_copy.start()

    taps_row = jnp.concatenate(
        [chirp[...].astype(F32), jnp.zeros((2, window - n_taps), F32)], axis=1
    )
    for part in range(2):
        spread = jnp.broadcast_to(taps_row[part : part + 1, :], (TILE, window))
        filt[part * TILE : (part + 1) * TILE, :] = pltpu.roll(
            spread, 0, 1, stride=1, stride_axis=0
        ).astype(BF16)

    beam_ids = lax.broadcasted_iota(jnp.int32, (beams, rows), 0)
    for level in range(levels):
        for child in range(2):
            tap = ktaps[level, child]
            real_w, imag_w = kweights[0, level, child], kweights[1, level, child]
            tap2 = jnp.concatenate([tap, tap], axis=1)
            upper_w = jnp.concatenate([real_w, imag_w], axis=1)
            lower_w = jnp.concatenate([-imag_w, real_w], axis=1)
            upper = jnp.zeros((beams, rows), F32)
            lower = jnp.zeros((beams, rows), F32)
            for t in range(tap.shape[0]):
                match = beam_ids == tap2[t : t + 1, :]
                upper = upper + jnp.where(match, upper_w[t : t + 1, :], 0.0)
                lower = lower + jnp.where(match, lower_w[t : t + 1, :], 0.0)
            kernels[level, child] = jnp.concatenate([upper, lower], axis=0).T.astype(BF16)
            row = mshift[level, child : child + 1, :]
            row2 = jnp.concatenate([row, row], axis=1) + REACH
            row_shift[level, child] = jnp.broadcast_to(row2, (rows, rows)).T

    phase_copy.wait()
    shift_copy.wait()

    def own_beams(own, got):
        stacked = jnp.concatenate([own, own, got, got], axis=0).T
        return jnp.where(sub == 0, stacked[:beams], stacked[beams:])

    angle = own_beams(phase[...], phases[...])
    lag = own_beams(shift[...], shifts[...])
    scale = 1.0 / math.sqrt(2 * local)
    cosine, sine = jnp.cos(angle) * scale, jnp.sin(angle) * scale
    is_real = lax.rem(lax.broadcasted_iota(jnp.int32, (beams, 4 * local), 1), 2 * local) < local
    upper = jnp.where(is_real, cosine, -sine)
    lower = jnp.where(is_real, sine, cosine)
    for index in range(offsets):
        match = lag == index - REACH
        select[index * rows : index * rows + beams, :] = jnp.where(match, upper, 0.0).astype(BF16)
        select[index * rows + beams : (index + 1) * rows, :] = jnp.where(
            match, lower, 0.0
        ).astype(BF16)

    own_copy.wait()

    @pl.when(rng > 0)
    def _():
        left_copy.wait_recv()

    for index in range(reach_devs):
        @pl.when(rng + index + 1 < n_rng)
        def _():
            right_copy(index).wait_recv()

    def valid(first, columns):
        bins = lax.broadcasted_iota(jnp.int32, (8, columns), 1) + (first - EDGE) + rng * slab
        return ((bins >= 0) & (bins < n_rng * slab))[0:1]

    for tile in range(width // TILE):
        first = tile * TILE
        data = cells[:, :, first : first + window].reshape(2 * local, window)
        both = lax.dot_general(
            data, filt[...], (((1,), (1,)), ((), ())), preferred_element_type=F32
        )
        keep = valid(first, TILE)
        real = both[:local, :TILE] + both[local:, TILE:]
        imag = both[local:, :TILE] - both[:local, TILE:]
        pulses[0, 0, :, first : first + TILE] = jnp.where(keep, real, 0.0).astype(BF16)
        pulses[0, 1, :, first : first + TILE] = jnp.where(keep, imag, 0.0).astype(BF16)

    pulse_copy = sub_copy(pulses.at[0], pulses.at[1], 2)
    pulse_copy.start()
    pulse_copy.wait()

    for tile in range(width // TILE):
        first = tile * TILE
        block = pulses[:, :, :, first : first + TILE].reshape(4 * local, TILE)
        products[:, first : first + TILE] = jnp.dot(
            select[...], block, preferred_element_type=F32
        )

    chunk = 16
    chunks = rows // chunk
    keep_all = valid(0, width)

    def level_copy(level, piece):
        return pltpu.make_async_remote_copy(
            src_ref=image.at[level, pl.ds(piece * chunk, chunk)],
            dst_ref=sibling.at[level, pl.ds(piece * chunk, chunk)],
            send_sem=lev_send.at[level * chunks + piece],
            recv_sem=lev_recv.at[level * chunks + piece],
            device_id={"aper": aper_partner(level)[0]},
            device_id_type=MESH,
        )

    for piece in range(chunks):
        for half in range(2):
            at = piece * chunk + half * 8
            total = jnp.zeros((8, width), F32)
            for index in range(offsets):
                part = products[index * rows + at : index * rows + at + 8, :]
                total = total + roll_left(part, index - REACH)
            products[at : at + 8, :] = jnp.where(keep_all, total, 0.0)
        image[0, piece * chunk : (piece + 1) * chunk, :] = products[
            piece * chunk : (piece + 1) * chunk, :
        ].astype(BF16)
        level_copy(0, piece).start()

    def moved(level, child_of, source):
        matrix = jnp.where(child_of == 0, kernels[level, 0], kernels[level, 1])
        by = jnp.where(child_of == 0, row_shift[level, 0], row_shift[level, 1])
        value = jnp.dot(matrix, source, preferred_element_type=F32)
        out_rows = []
        for first in range(0, rows, 8):
            part = value[first : first + 8]
            lanes = by[first : first + 8, 0:1]
            bit = 1
            while bit <= 2 * REACH:
                part = jnp.where((lanes & bit) != 0, roll_left(part, bit), part)
                bit *= 2
            out_rows.append(part)
        return out_rows

    for level in range(levels):
        side = aper_partner(level)[1]
        own = moved(level, side, image[level])
        for first in range(0, rows, 8):
            products[first : first + 8, :] = own[first // 8]
        for piece in range(chunks):
            level_copy(level, piece).wait_recv()
        other = moved(level, 1 - side, sibling[level])
        for piece in range(chunks):
            at = piece * chunk
            merged = jnp.concatenate(
                [
                    jnp.where(
                        keep_all,
                        roll_left(products[a : a + 8, :] + other[a // 8], -REACH),
                        0.0,
                    )
                    for a in (at, at + 8)
                ],
                axis=0,
            ).astype(BF16)
            if level < levels - 1:
                image[level + 1, at : at + chunk, :] = merged
                level_copy(level + 1, piece).start()
            else:
                out[at // beams, at % beams : at % beams + chunk, :] = merged[
                    :, EDGE : EDGE + slab
                ]

    pl_levels = range(levels)
    for level in pl_levels:
        for piece in range(chunks):
            level_copy(level, piece).wait_send()
    for index in range(reach_devs):
        @pl.when(rng >= index + 1)
        def _():
            right_copy(index).wait_send()

    @pl.when(rng + 1 < n_rng)
    def _():
        left_copy.wait_send()


def shards(n_rng, n_aper, echoes, chirp, phase, shift, ktaps, mshift, kweights):
    local, slab = echoes.shape[1], echoes.shape[2]
    n_taps = chirp.shape[1]
    beams = ktaps.shape[3]
    rows = 2 * beams
    levels = n_aper.bit_length() - 1
    width = slab + 2 * EDGE
    need = n_taps + EDGE
    halos = []
    while need > 0:
        halos.append(min(slab, need))
        need -= slab
    halo = n_taps + EDGE
    offsets = 2 * REACH + 1
    pieces = levels * (rows // 16)
    vmem = pl.BlockSpec(memory_space=pltpu.VMEM)
    return pl.pallas_call(
        functools.partial(image_kernel, n_rng, n_aper, levels, tuple(halos)),
        out_shape=jax.ShapeDtypeStruct((2, beams, slab), BF16),
        in_specs=[pl.BlockSpec(memory_space=pl.ANY)] + [vmem] * 6,
        out_specs=vmem,
        scratch_shapes=[
            pltpu.VMEM((2, local, EDGE + slab + halo), BF16),
            pltpu.VMEM((2 * TILE, TILE + n_taps), BF16),
            pltpu.VMEM(phase.shape, F32),
            pltpu.VMEM(shift.shape, jnp.int32),
            pltpu.VMEM((offsets * rows, 4 * local), BF16),
            pltpu.VMEM((2, 2, local, width), BF16),
            pltpu.VMEM((offsets * rows, width), F32),
            pltpu.VMEM((levels, rows, width), BF16),
            pltpu.VMEM((levels, rows, width), BF16),
            pltpu.VMEM((levels, 2, rows, rows), BF16),
            pltpu.VMEM((levels, 2, rows, rows), jnp.int32),
            pltpu.SemaphoreType.DMA,
            pltpu.SemaphoreType.DMA((len(halos) + 1,)),
            pltpu.SemaphoreType.DMA((len(halos) + 1,)),
            pltpu.SemaphoreType.DMA((3,)),
            pltpu.SemaphoreType.DMA((3,)),
            pltpu.SemaphoreType.DMA((pieces,)),
            pltpu.SemaphoreType.DMA((pieces,)),
        ],
        compiler_params=pltpu.CompilerParams(
            collective_id=0, has_side_effects=True, vmem_limit_bytes=40 * 2**20
        ),
    )(echoes, chirp, phase, shift, ktaps, mshift, kweights)


def solution(mesh):
    placed = (
        P(None, ("parts", "aper", "sub"), "rng"),
        P(),
        P(("parts", "aper", "sub"), None),
        P(("parts", "aper", "sub"), None),
        P(None, None, None, ("parts", "aper", "sub")),
        P(None, None, ("parts", "aper", "sub")),
        P(None, None, None, None, ("parts", "aper", "sub")),
    )
    return jax.shard_map(
        functools.partial(shards, mesh.shape["rng"], mesh.shape["aper"]),
        mesh=mesh,
        in_specs=placed,
        out_specs=P(None, ("parts", "aper", "sub"), "rng"),
        check_vma=False,
    )
```

```python
import functools
import math

import jax
import jax.numpy as jnp
from jax import lax
from jax.experimental import pallas as pl
from jax.experimental.pallas import tpu as pltpu
from jax.sharding import PartitionSpec as P

REACH = 8
EDGE = 128
HALF = EDGE // 2
TILE = 256
MESH = pl.DeviceIdType.MESH
F32 = jnp.float32
BF16 = jnp.bfloat16


def roll_left(value, by):
    width = value.shape[1]
    by = by % width
    return value if by == 0 else pltpu.roll(value, width - by, 1)


def image_kernel(
    n_rng, n_aper, levels, halos,
    echoes, chirp, phase_in, shift_in, ktaps_in, mshift_in, kweights_in,
    out,
    phase, shift, ktaps, mshift, kweights, cells, filt, phases, shifts, select, pulses, products, image, sibling, kernels, row_shift,
    own_sem, halo_send, halo_recv, sub_send, sub_recv, lev_send, lev_recv,
):
    rng = lax.axis_index("rng")
    aper = lax.axis_index("aper")
    sub = lax.axis_index("sub")
    local, slab = echoes.shape[1], echoes.shape[2]
    n_taps = chirp.shape[1]
    beams = out.shape[1]
    rows = 2 * beams
    width = slab + 2 * EDGE
    window = TILE + n_taps
    offsets = 2 * REACH + 1
    reach_devs = halos[-1][0]
    circle = slab + EDGE
    left_index = len(halos)

    barrier = pltpu.get_barrier_semaphore()
    pl.semaphore_signal(barrier, inc=1, device_id={"sub": 1 - sub}, device_id_type=MESH)

    def aper_partner(level):
        stride = 2**level
        side = lax.rem(aper // stride, 2)
        return aper + stride - 2 * stride * side, side

    for level in range(levels):
        pl.semaphore_signal(
            barrier, inc=1, device_id={"aper": aper_partner(level)[0]}, device_id_type=MESH
        )
    for dist in range(1, reach_devs + 1):
        @pl.when(rng + dist < n_rng)
        def _():
            pl.semaphore_signal(barrier, inc=1, device_id={"rng": rng + dist}, device_id_type=MESH)

        @pl.when(rng >= dist)
        def _():
            pl.semaphore_signal(barrier, inc=1, device_id={"rng": rng - dist}, device_id_type=MESH)

    own_copy = pltpu.make_async_copy(echoes, cells.at[:, :, pl.ds(EDGE, slab)], own_sem.at[0])
    own_copy.start()
    tables = ((phase_in, phase), (shift_in, shift), (ktaps_in, ktaps), (mshift_in, mshift),
              (kweights_in, kweights))
    loads = [
        pltpu.make_async_copy(src, dst, own_sem.at[1 + i]) for i, (src, dst) in enumerate(tables)
    ]
    for load in loads:
        load.start()
    if reach_devs >= n_rng - 1:
        rng_peers = n_rng - 1
    else:
        rng_peers = jnp.minimum(rng, reach_devs) + jnp.minimum(n_rng - 1 - rng, reach_devs)
    pl.semaphore_wait(barrier, 1 + levels + rng_peers)

    def right_copy(index):
        dist, start, count = halos[index]
        return pltpu.make_async_remote_copy(
            src_ref=echoes.at[:, :, pl.ds(start, count)],
            dst_ref=cells.at[:, :, pl.ds(EDGE + dist * slab + start, count)],
            send_sem=halo_send.at[index],
            recv_sem=halo_recv.at[index],
            device_id={"rng": rng - dist},
            device_id_type=MESH,
        )

    left_copy = pltpu.make_async_remote_copy(
        src_ref=echoes.at[:, :, pl.ds(slab - EDGE, EDGE)],
        dst_ref=cells.at[:, :, pl.ds(0, EDGE)],
        send_sem=halo_send.at[left_index],
        recv_sem=halo_recv.at[left_index],
        device_id={"rng": rng + 1},
        device_id_type=MESH,
    )
    for index, (dist, start, count) in enumerate(halos):
        @pl.when(rng >= dist)
        def _():
            right_copy(index).start()

        @pl.when(rng + dist >= n_rng)
        def _():
            first = EDGE + dist * slab + start
            cells[:, :, first : first + count] = jnp.zeros((2, local, count), BF16)

    @pl.when(rng + 1 < n_rng)
    def _():
        left_copy.start()

    @pl.when(rng == 0)
    def _():
        cells[:, :, 0:EDGE] = jnp.zeros((2, local, EDGE), BF16)

    def sub_copy(src, dst, index):
        return pltpu.make_async_remote_copy(
            src_ref=src,
            dst_ref=dst,
            send_sem=sub_send.at[index],
            recv_sem=sub_recv.at[index],
            device_id={"sub": 1 - sub},
            device_id_type=MESH,
        )

    phase_copy = sub_copy(phase_in, phases, 0)
    shift_copy = sub_copy(shift_in, shifts, 1)
    phase_copy.start()
    shift_copy.start()

    taps_row = jnp.concatenate(
        [chirp[...].astype(F32), jnp.zeros((2, window - n_taps), F32)], axis=1
    )
    for part in range(2):
        spread = jnp.broadcast_to(taps_row[part : part + 1, :], (TILE, window))
        filt[part * TILE : (part + 1) * TILE, :] = pltpu.roll(
            spread, 0, 1, stride=1, stride_axis=0
        ).astype(BF16)

    for load in loads:
        load.wait()

    beam_ids = lax.broadcasted_iota(jnp.int32, (beams, rows), 0)
    for level in range(levels):
        for child in range(2):
            tap = ktaps[level, child]
            real_w, imag_w = kweights[0, level, child], kweights[1, level, child]
            tap2 = jnp.concatenate([tap, tap], axis=1)
            upper_w = jnp.concatenate([real_w, imag_w], axis=1)
            lower_w = jnp.concatenate([-imag_w, real_w], axis=1)
            upper = jnp.zeros((beams, rows), F32)
            lower = jnp.zeros((beams, rows), F32)
            for t in range(tap.shape[0]):
                match = beam_ids == tap2[t : t + 1, :]
                upper = upper + jnp.where(match, upper_w[t : t + 1, :], 0.0)
                lower = lower + jnp.where(match, lower_w[t : t + 1, :], 0.0)
            kernels[level, child] = jnp.concatenate([upper, lower], axis=0).T.astype(BF16)
            row = mshift[level, child : child + 1, :]
            row2 = jnp.concatenate([row, row], axis=1) + REACH
            row_shift[level, child] = jnp.broadcast_to(row2, (rows, rows)).T

    phase_copy.wait()
    shift_copy.wait()

    def own_beams(own, got):
        stacked = jnp.concatenate([own, own, got, got], axis=0).T
        return jnp.where(sub == 0, stacked[:beams], stacked[beams:])

    angle = own_beams(phase[...], phases[...])
    lag = own_beams(shift[...], shifts[...])
    scale = 1.0 / math.sqrt(2 * local)
    cosine, sine = jnp.cos(angle) * scale, jnp.sin(angle) * scale
    is_real = lax.rem(lax.broadcasted_iota(jnp.int32, (beams, 4 * local), 1), 2 * local) < local
    upper = jnp.where(is_real, cosine, -sine)
    lower = jnp.where(is_real, sine, cosine)
    for index in range(offsets):
        match = lag == index - REACH
        select[index * rows : index * rows + beams, :] = jnp.where(match, upper, 0.0).astype(BF16)
        select[index * rows + beams : (index + 1) * rows, :] = jnp.where(
            match, lower, 0.0
        ).astype(BF16)

    own_copy.wait()

    def valid(first, columns):
        bins = lax.broadcasted_iota(jnp.int32, (8, columns), 1) + (first - EDGE) + rng * slab
        return ((bins >= 0) & (bins < n_rng * slab))[0:1]

    tiles = width // TILE
    order = list(range(1, tiles))
    order.insert(1, 0)

    def pulse_copy(tile):
        at = pl.ds(tile * TILE, TILE)
        return sub_copy(pulses.at[0, :, :, at], pulses.at[1, :, :, at], 2 + tile)

    arrived = 0
    for tile in order:
        first = tile * TILE
        if tile == 0:
            @pl.when(rng > 0)
            def _():
                left_copy.wait_recv()
        while arrived < len(halos):
            dist, start, count = halos[arrived]
            if EDGE + dist * slab + start >= first + window:
                break

            @pl.when(rng + dist < n_rng)
            def _():
                right_copy(arrived).wait_recv()

            arrived += 1
        data = cells[:, :, first : first + window].reshape(2 * local, window)
        both = lax.dot_general(
            data, filt[...], (((1,), (1,)), ((), ())), preferred_element_type=F32
        )
        keep = valid(first, TILE)
        real = both[:local, :TILE] + both[local:, TILE:]
        imag = both[local:, :TILE] - both[:local, TILE:]
        pulses[0, 0, :, first : first + TILE] = jnp.where(keep, real, 0.0).astype(BF16)
        pulses[0, 1, :, first : first + TILE] = jnp.where(keep, imag, 0.0).astype(BF16)
        pulse_copy(tile).start()

    for tile in order:
        first = tile * TILE
        pulse_copy(tile).wait_recv()
        block = pulses[:, :, :, first : first + TILE].reshape(4 * local, TILE)
        products[:, first : first + TILE] = jnp.dot(
            select[...], block, preferred_element_type=F32
        )

    chunk = 16
    chunks = rows // chunk
    column = lax.broadcasted_iota(jnp.int32, (8, circle), 1)
    bins = jnp.where(column < slab + HALF, column, column - circle) + rng * slab
    keep_all = ((bins >= 0) & (bins < n_rng * slab))[0:1]
    is_next = lax.broadcasted_iota(jnp.int32, (8, EDGE), 1) < HALF

    def level_copy(level, piece):
        return pltpu.make_async_remote_copy(
            src_ref=image.at[level, pl.ds(piece * chunk, chunk)],
            dst_ref=sibling.at[level, pl.ds(piece * chunk, chunk)],
            send_sem=lev_send.at[level * chunks + piece],
            recv_sem=lev_recv.at[level * chunks + piece],
            device_id={"aper": aper_partner(level)[0]},
            device_id_type=MESH,
        )

    for piece in range(chunks):
        for half in range(2):
            at = piece * chunk + half * 8
            total = jnp.zeros((8, circle), F32)
            for index in range(offsets):
                here = index * rows + at
                margin = jnp.where(
                    is_next,
                    products[here : here + 8, EDGE + slab :],
                    products[here : here + 8, :EDGE],
                )
                part = jnp.concatenate(
                    [products[here : here + 8, EDGE : EDGE + slab], margin], axis=1
                )
                total = total + roll_left(part, index - REACH)
            products[at : at + 8, :circle] = jnp.where(keep_all, total, 0.0)
        image[0, piece * chunk : (piece + 1) * chunk, :] = products[
            piece * chunk : (piece + 1) * chunk, :circle
        ].astype(BF16)
        level_copy(0, piece).start()

    def moved(level, child_of, source):
        matrix = jnp.where(child_of == 0, kernels[level, 0], kernels[level, 1])
        by = jnp.where(child_of == 0, row_shift[level, 0], row_shift[level, 1])
        value = jnp.dot(matrix, source, preferred_element_type=F32)
        out_rows = []
        for first in range(0, rows, 8):
            part = value[first : first + 8]
            lanes = by[first : first + 8, 0:1]
            bit = 1
            while bit <= 2 * REACH:
                part = jnp.where((lanes & bit) != 0, roll_left(part, bit), part)
                bit *= 2
            out_rows.append(part)
        return out_rows

    for level in range(levels):
        side = aper_partner(level)[1]
        own = moved(level, side, image[level])
        for first in range(0, rows, 8):
            products[first : first + 8, :circle] = own[first // 8]
        for piece in range(chunks):
            level_copy(level, piece).wait_recv()
        other = moved(level, 1 - side, sibling[level])
        for piece in range(chunks):
            at = piece * chunk
            merged = jnp.concatenate(
                [
                    jnp.where(
                        keep_all,
                        roll_left(products[a : a + 8, :circle] + other[a // 8], -REACH),
                        0.0,
                    )
                    for a in (at, at + 8)
                ],
                axis=0,
            ).astype(BF16)
            if level < levels - 1:
                image[level + 1, at : at + chunk, :] = merged
                level_copy(level + 1, piece).start()
            else:
                out[at // beams, at % beams : at % beams + chunk, :] = merged[
                    :, :slab
                ]

    pl_levels = range(levels)
    for level in pl_levels:
        for piece in range(chunks):
            level_copy(level, piece).wait_send()
    for tile in order:
        pulse_copy(tile).wait_send()
    for index, (dist, _, _) in enumerate(halos):
        @pl.when(rng >= dist)
        def _():
            right_copy(index).wait_send()

    @pl.when(rng + 1 < n_rng)
    def _():
        left_copy.wait_send()


def shards(n_rng, n_aper, echoes, chirp, phase, shift, ktaps, mshift, kweights):
    local, slab = echoes.shape[1], echoes.shape[2]
    n_taps = chirp.shape[1]
    beams = ktaps.shape[3]
    rows = 2 * beams
    levels = n_aper.bit_length() - 1
    width = slab + 2 * EDGE
    halos = []
    at = 0
    while at < n_taps + EDGE:
        ends = ((at + EDGE) // TILE * TILE + EDGE, (at // slab + 1) * slab, n_taps + EDGE)
        end = min(e for e in ends if e > at)
        halos.append((at // slab + 1, at % slab, end - at))
        at = end
    halo = n_taps + EDGE
    offsets = 2 * REACH + 1
    pieces = levels * (rows // 16)
    vmem = pl.BlockSpec(memory_space=pltpu.VMEM)
    hbm = pl.BlockSpec(memory_space=pltpu.HBM)
    tables = (phase, shift, ktaps, mshift, kweights)
    return pl.pallas_call(
        functools.partial(image_kernel, n_rng, n_aper, levels, tuple(halos)),
        out_shape=jax.ShapeDtypeStruct((2, beams, slab), BF16),
        in_specs=[hbm, vmem] + [hbm] * 5,
        out_specs=vmem,
        scratch_shapes=[pltpu.VMEM(t.shape, t.dtype) for t in tables] + [
            pltpu.VMEM((2, local, EDGE + slab + halo), BF16),
            pltpu.VMEM((2 * TILE, TILE + n_taps), BF16),
            pltpu.VMEM(phase.shape, F32),
            pltpu.VMEM(shift.shape, jnp.int32),
            pltpu.VMEM((offsets * rows, 4 * local), BF16),
            pltpu.VMEM((2, 2, local, width), BF16),
            pltpu.VMEM((offsets * rows, width), F32),
            pltpu.VMEM((levels, rows, slab + EDGE), BF16),
            pltpu.VMEM((levels, rows, slab + EDGE), BF16),
            pltpu.VMEM((levels, 2, rows, rows), BF16),
            pltpu.VMEM((levels, 2, rows, rows), jnp.int32),
            pltpu.SemaphoreType.DMA((6,)),
            pltpu.SemaphoreType.DMA((len(halos) + 1,)),
            pltpu.SemaphoreType.DMA((len(halos) + 1,)),
            pltpu.SemaphoreType.DMA((2 + width // TILE,)),
            pltpu.SemaphoreType.DMA((2 + width // TILE,)),
            pltpu.SemaphoreType.DMA((pieces,)),
            pltpu.SemaphoreType.DMA((pieces,)),
        ],
        compiler_params=pltpu.CompilerParams(
            collective_id=0, has_side_effects=True, vmem_limit_bytes=64 * 2**20 - 2**17
        ),
    )(echoes, chirp, phase, shift, ktaps, mshift, kweights)


def solution(mesh):
    placed = (
        P(None, ("parts", "aper", "sub"), "rng"),
        P(),
        P(("parts", "aper", "sub"), None),
        P(("parts", "aper", "sub"), None),
        P(None, None, None, ("parts", "aper", "sub")),
        P(None, None, ("parts", "aper", "sub")),
        P(None, None, None, None, ("parts", "aper", "sub")),
    )
    return jax.shard_map(
        functools.partial(shards, mesh.shape["rng"], mesh.shape["aper"]),
        mesh=mesh,
        in_specs=placed,
        out_specs=P(None, ("parts", "aper", "sub"), "rng"),
        check_vma=False,
    )
```

```python
import functools
import math

import jax
import jax.numpy as jnp
from jax import lax
from jax.experimental import pallas as pl
from jax.experimental.pallas import tpu as pltpu
from jax.sharding import PartitionSpec as P

REACH = 8
EDGE = 128
HALF = EDGE // 2
TILE = 256
MESH = pl.DeviceIdType.MESH
F32 = jnp.float32
BF16 = jnp.bfloat16


def roll_left(value, by):
    width = value.shape[1]
    by = by % width
    return value if by == 0 else pltpu.roll(value, width - by, 1)


def image_kernel(
    n_rng, n_aper, levels, halos,
    echoes, chirp, phase_in, shift_in, ktaps_in, mshift_in, kweights_in,
    out,
    phase, shift, ktaps, mshift, kweights, cells, filt, phases, shifts, select, pulses, products, image, sibling, kernels, row_shift,
    own_sem, halo_send, halo_recv, sub_send, sub_recv, lev_send, lev_recv,
):
    rng = lax.axis_index("rng")
    aper = lax.axis_index("aper")
    sub = lax.axis_index("sub")
    local, slab = echoes.shape[1], echoes.shape[2]
    n_taps = chirp.shape[1]
    beams = out.shape[1]
    rows = 2 * beams
    width = slab + 2 * EDGE
    window = TILE + n_taps
    offsets = 2 * REACH + 1
    chunk = 16
    chunks = rows // chunk
    reach_devs = halos[-1][0]
    circle = slab + EDGE
    left_index = len(halos)

    barrier = pltpu.get_barrier_semaphore()
    pl.semaphore_signal(barrier, inc=1, device_id={"sub": 1 - sub}, device_id_type=MESH)

    def aper_partner(level):
        stride = 2**level
        side = lax.rem(aper // stride, 2)
        return aper + stride - 2 * stride * side, side

    for level in range(levels):
        pl.semaphore_signal(
            barrier, inc=1, device_id={"aper": aper_partner(level)[0]}, device_id_type=MESH
        )
    for dist in range(1, reach_devs + 1):
        @pl.when(rng + dist < n_rng)
        def _():
            pl.semaphore_signal(barrier, inc=1, device_id={"rng": rng + dist}, device_id_type=MESH)

        @pl.when(rng >= dist)
        def _():
            pl.semaphore_signal(barrier, inc=1, device_id={"rng": rng - dist}, device_id_type=MESH)

    own_copy = pltpu.make_async_copy(echoes, cells.at[:, :, pl.ds(EDGE, slab)], own_sem.at[0])
    own_copy.start()
    tables = ((phase_in, phase), (shift_in, shift), (ktaps_in, ktaps), (mshift_in, mshift),
              (kweights_in, kweights))
    loads = [
        pltpu.make_async_copy(src, dst, own_sem.at[1 + i]) for i, (src, dst) in enumerate(tables)
    ]
    for load in loads:
        load.start()
    if reach_devs >= n_rng - 1:
        rng_peers = n_rng - 1
    else:
        rng_peers = jnp.minimum(rng, reach_devs) + jnp.minimum(n_rng - 1 - rng, reach_devs)
    pl.semaphore_wait(barrier, 1 + levels + rng_peers)

    def right_copy(index):
        dist, start, count = halos[index]
        return pltpu.make_async_remote_copy(
            src_ref=echoes.at[:, :, pl.ds(start, count)],
            dst_ref=cells.at[:, :, pl.ds(EDGE + dist * slab + start, count)],
            send_sem=halo_send.at[index],
            recv_sem=halo_recv.at[index],
            device_id={"rng": rng - dist},
            device_id_type=MESH,
        )

    left_copy = pltpu.make_async_remote_copy(
        src_ref=echoes.at[:, :, pl.ds(slab - EDGE, EDGE)],
        dst_ref=cells.at[:, :, pl.ds(0, EDGE)],
        send_sem=halo_send.at[left_index],
        recv_sem=halo_recv.at[left_index],
        device_id={"rng": rng + 1},
        device_id_type=MESH,
    )
    for index, (dist, start, count) in enumerate(halos):
        @pl.when(rng >= dist)
        def _():
            right_copy(index).start()

        @pl.when(rng + dist >= n_rng)
        def _():
            first = EDGE + dist * slab + start
            cells[:, :, first : first + count] = jnp.zeros((2, local, count), BF16)

    @pl.when(rng + 1 < n_rng)
    def _():
        left_copy.start()

    @pl.when(rng == 0)
    def _():
        cells[:, :, 0:EDGE] = jnp.zeros((2, local, EDGE), BF16)

    def sub_copy(src, dst, index):
        return pltpu.make_async_remote_copy(
            src_ref=src,
            dst_ref=dst,
            send_sem=sub_send.at[index],
            recv_sem=sub_recv.at[index],
            device_id={"sub": 1 - sub},
            device_id_type=MESH,
        )

    phase_copy = sub_copy(phase_in, phases, 0)
    shift_copy = sub_copy(shift_in, shifts, 1)
    phase_copy.start()
    shift_copy.start()

    taps_row = jnp.concatenate(
        [chirp[...].astype(F32), jnp.zeros((2, window - n_taps), F32)], axis=1
    )
    for part in range(2):
        spread = jnp.broadcast_to(taps_row[part : part + 1, :], (TILE, window))
        filt[part * TILE : (part + 1) * TILE, :] = pltpu.roll(
            spread, 0, 1, stride=1, stride_axis=0
        ).astype(BF16)

    for load in loads:
        load.wait()

    beam_ids = lax.broadcasted_iota(jnp.int32, (beams, rows), 0)
    for level in range(levels):
        for child in range(2):
            tap = ktaps[level, child]
            real_w, imag_w = kweights[0, level, child], kweights[1, level, child]
            tap2 = jnp.concatenate([tap, tap], axis=1)
            upper_w = jnp.concatenate([real_w, imag_w], axis=1)
            lower_w = jnp.concatenate([-imag_w, real_w], axis=1)
            upper = jnp.zeros((beams, rows), F32)
            lower = jnp.zeros((beams, rows), F32)
            for t in range(tap.shape[0]):
                match = beam_ids == tap2[t : t + 1, :]
                upper = upper + jnp.where(match, upper_w[t : t + 1, :], 0.0)
                lower = lower + jnp.where(match, lower_w[t : t + 1, :], 0.0)
            kernels[level, child] = jnp.concatenate([upper, lower], axis=0).T.astype(BF16)
            row = mshift[level, child : child + 1, :]
            row2 = jnp.concatenate([row, row], axis=1) + REACH
            row_shift[level, child] = jnp.broadcast_to(row2, (rows, rows)).T

    phase_copy.wait()
    shift_copy.wait()

    def own_beams(own, got):
        stacked = jnp.concatenate([own, own, got, got], axis=0).T
        return jnp.where(sub == 0, stacked[:beams], stacked[beams:])

    angle = own_beams(phase[...], phases[...])
    lag = own_beams(shift[...], shifts[...])
    scale = 1.0 / math.sqrt(2 * local)
    cosine, sine = jnp.cos(angle) * scale, jnp.sin(angle) * scale
    is_real = lax.rem(lax.broadcasted_iota(jnp.int32, (beams, 4 * local), 1), 2 * local) < local
    upper = jnp.where(is_real, cosine, -sine)
    lower = jnp.where(is_real, sine, cosine)
    for index in range(offsets):
        match = lag == index - REACH
        both = jnp.concatenate(
            [jnp.where(match, upper, 0.0), jnp.where(match, lower, 0.0)], axis=0
        ).astype(BF16)
        for piece in range(chunks):
            here = (piece * offsets + index) * chunk
            select[here : here + chunk, :] = both[piece * chunk : (piece + 1) * chunk]

    own_copy.wait()

    def valid(first, columns):
        bins = lax.broadcasted_iota(jnp.int32, (8, columns), 1) + (first - EDGE) + rng * slab
        return ((bins >= 0) & (bins < n_rng * slab))[0:1]

    tiles = width // TILE
    order = list(range(1, tiles))
    order.insert(1, 0)

    def pulse_copy(tile):
        at = pl.ds(tile * TILE, TILE)
        return sub_copy(pulses.at[0, :, :, at], pulses.at[1, :, :, at], 2 + tile)

    arrived = 0
    for tile in order:
        first = tile * TILE
        if tile == 0:
            @pl.when(rng > 0)
            def _():
                left_copy.wait_recv()
        while arrived < len(halos):
            dist, start, count = halos[arrived]
            if EDGE + dist * slab + start >= first + window:
                break

            @pl.when(rng + dist < n_rng)
            def _():
                right_copy(arrived).wait_recv()

            arrived += 1
        data = cells[:, :, first : first + window].reshape(2 * local, window)
        both = lax.dot_general(
            data, filt[...], (((1,), (1,)), ((), ())), preferred_element_type=F32
        )
        keep = valid(first, TILE)
        real = both[:local, :TILE] + both[local:, TILE:]
        imag = both[local:, :TILE] - both[:local, TILE:]
        pulses[0, 0, :, first : first + TILE] = jnp.where(keep, real, 0.0).astype(BF16)
        pulses[0, 1, :, first : first + TILE] = jnp.where(keep, imag, 0.0).astype(BF16)
        pulse_copy(tile).start()

    column = lax.broadcasted_iota(jnp.int32, (8, circle), 1)
    bins = jnp.where(column < slab + HALF, column, column - circle) + rng * slab
    keep_all = ((bins >= 0) & (bins < n_rng * slab))[0:1]
    is_next = lax.broadcasted_iota(jnp.int32, (8, EDGE), 1) < HALF

    def level_copy(level, piece):
        return pltpu.make_async_remote_copy(
            src_ref=image.at[level, pl.ds(piece * chunk, chunk)],
            dst_ref=sibling.at[level, pl.ds(piece * chunk, chunk)],
            send_sem=lev_send.at[level * chunks + piece],
            recv_sem=lev_recv.at[level * chunks + piece],
            device_id={"aper": aper_partner(level)[0]},
            device_id_type=MESH,
        )

    for piece in range(chunks):
        group = slice(piece * offsets * chunk, (piece + 1) * offsets * chunk)
        for tile in order:
            first = tile * TILE
            if piece == 0:
                pulse_copy(tile).wait_recv()
            block = pulses[:, :, :, first : first + TILE].reshape(4 * local, TILE)
            products[group, first : first + TILE] = jnp.dot(
                select[group, :], block, preferred_element_type=F32
            )
        for half in range(2):
            at = piece * chunk + half * 8
            total = jnp.zeros((8, circle), F32)
            for index in range(offsets):
                here = (piece * offsets + index) * chunk + half * 8
                margin = jnp.where(
                    is_next,
                    products[here : here + 8, EDGE + slab :],
                    products[here : here + 8, :EDGE],
                )
                part = jnp.concatenate(
                    [products[here : here + 8, EDGE : EDGE + slab], margin], axis=1
                )
                total = total + roll_left(part, index - REACH)
            products[at : at + 8, :circle] = jnp.where(keep_all, total, 0.0)
        image[0, piece * chunk : (piece + 1) * chunk, :] = products[
            piece * chunk : (piece + 1) * chunk, :circle
        ].astype(BF16)
        level_copy(0, piece).start()

    def moved(level, child_of, source):
        matrix = jnp.where(child_of == 0, kernels[level, 0], kernels[level, 1])
        by = jnp.where(child_of == 0, row_shift[level, 0], row_shift[level, 1])
        value = jnp.dot(matrix, source, preferred_element_type=F32)
        out_rows = []
        for first in range(0, rows, 8):
            part = value[first : first + 8]
            lanes = by[first : first + 8, 0:1]
            bit = 1
            while bit <= 2 * REACH:
                part = jnp.where((lanes & bit) != 0, roll_left(part, bit), part)
                bit *= 2
            out_rows.append(part)
        return out_rows

    for level in range(levels):
        side = aper_partner(level)[1]
        own = moved(level, side, image[level])
        for first in range(0, rows, 8):
            products[first : first + 8, :circle] = own[first // 8]
        for piece in range(chunks):
            level_copy(level, piece).wait_recv()
        other = moved(level, 1 - side, sibling[level])
        for piece in range(chunks):
            at = piece * chunk
            merged = jnp.concatenate(
                [
                    jnp.where(
                        keep_all,
                        roll_left(products[a : a + 8, :circle] + other[a // 8], -REACH),
                        0.0,
                    )
                    for a in (at, at + 8)
                ],
                axis=0,
            ).astype(BF16)
            if level < levels - 1:
                image[level + 1, at : at + chunk, :] = merged
                level_copy(level + 1, piece).start()
            else:
                out[at // beams, at % beams : at % beams + chunk, :] = merged[
                    :, :slab
                ]

    pl_levels = range(levels)
    for level in pl_levels:
        for piece in range(chunks):
            level_copy(level, piece).wait_send()
    for tile in order:
        pulse_copy(tile).wait_send()
    for index, (dist, _, _) in enumerate(halos):
        @pl.when(rng >= dist)
        def _():
            right_copy(index).wait_send()

    @pl.when(rng + 1 < n_rng)
    def _():
        left_copy.wait_send()


def shards(n_rng, n_aper, echoes, chirp, phase, shift, ktaps, mshift, kweights):
    local, slab = echoes.shape[1], echoes.shape[2]
    n_taps = chirp.shape[1]
    beams = ktaps.shape[3]
    rows = 2 * beams
    levels = n_aper.bit_length() - 1
    width = slab + 2 * EDGE
    halos = []
    at = 0
    while at < n_taps + EDGE:
        ends = ((at + EDGE) // TILE * TILE + EDGE, (at // slab + 1) * slab, n_taps + EDGE)
        end = min(e for e in ends if e > at)
        halos.append((at // slab + 1, at % slab, end - at))
        at = end
    halo = n_taps + EDGE
    offsets = 2 * REACH + 1
    pieces = levels * (rows // 16)
    vmem = pl.BlockSpec(memory_space=pltpu.VMEM)
    hbm = pl.BlockSpec(memory_space=pltpu.HBM)
    tables = (phase, shift, ktaps, mshift, kweights)
    return pl.pallas_call(
        functools.partial(image_kernel, n_rng, n_aper, levels, tuple(halos)),
        out_shape=jax.ShapeDtypeStruct((2, beams, slab), BF16),
        in_specs=[hbm, vmem] + [hbm] * 5,
        out_specs=vmem,
        scratch_shapes=[pltpu.VMEM(t.shape, t.dtype) for t in tables] + [
            pltpu.VMEM((2, local, EDGE + slab + halo), BF16),
            pltpu.VMEM((2 * TILE, TILE + n_taps), BF16),
            pltpu.VMEM(phase.shape, F32),
            pltpu.VMEM(shift.shape, jnp.int32),
            pltpu.VMEM((offsets * rows, 4 * local), BF16),
            pltpu.VMEM((2, 2, local, width), BF16),
            pltpu.VMEM((offsets * rows, width), F32),
            pltpu.VMEM((levels, rows, slab + EDGE), BF16),
            pltpu.VMEM((levels, rows, slab + EDGE), BF16),
            pltpu.VMEM((levels, 2, rows, rows), BF16),
            pltpu.VMEM((levels, 2, rows, rows), jnp.int32),
            pltpu.SemaphoreType.DMA((6,)),
            pltpu.SemaphoreType.DMA((len(halos) + 1,)),
            pltpu.SemaphoreType.DMA((len(halos) + 1,)),
            pltpu.SemaphoreType.DMA((2 + width // TILE,)),
            pltpu.SemaphoreType.DMA((2 + width // TILE,)),
            pltpu.SemaphoreType.DMA((pieces,)),
            pltpu.SemaphoreType.DMA((pieces,)),
        ],
        compiler_params=pltpu.CompilerParams(
            collective_id=0, has_side_effects=True, vmem_limit_bytes=64 * 2**20 - 2**17
        ),
    )(echoes, chirp, phase, shift, ktaps, mshift, kweights)


def solution(mesh):
    placed = (
        P(None, ("parts", "aper", "sub"), "rng"),
        P(),
        P(("parts", "aper", "sub"), None),
        P(("parts", "aper", "sub"), None),
        P(None, None, None, ("parts", "aper", "sub")),
        P(None, None, ("parts", "aper", "sub")),
        P(None, None, None, None, ("parts", "aper", "sub")),
    )
    return jax.shard_map(
        functools.partial(shards, mesh.shape["rng"], mesh.shape["aper"]),
        mesh=mesh,
        in_specs=placed,
        out_specs=P(None, ("parts", "aper", "sub"), "rng"),
        check_vma=False,
    )
```

```python
import functools
import math

import jax
import jax.numpy as jnp
from jax import lax
from jax.experimental import pallas as pl
from jax.experimental.pallas import tpu as pltpu
from jax.sharding import PartitionSpec as P

REACH = 8
EDGE = 128
HALF = EDGE // 2
TILE = 256
MESH = pl.DeviceIdType.MESH
F32 = jnp.float32
BF16 = jnp.bfloat16


def roll_left(value, by):
    width = value.shape[1]
    by = by % width
    return value if by == 0 else pltpu.roll(value, width - by, 1)


def image_kernel(
    n_rng, n_aper, levels, halos,
    echoes, chirp, phase_in, shift_in, ktaps_in, mshift_in, kweights_in,
    out,
    phase, shift, ktaps, mshift, kweights, cells, filt, phases, shifts, select, pulses, products, image, sibling, kernels, row_shift,
    own_sem, halo_send, halo_recv, sub_send, sub_recv, lev_send, lev_recv,
):
    rng = lax.axis_index("rng")
    aper = lax.axis_index("aper")
    sub = lax.axis_index("sub")
    local, slab = echoes.shape[1], echoes.shape[2]
    n_taps = chirp.shape[1]
    beams = out.shape[1]
    rows = 2 * beams
    width = slab + 2 * EDGE
    window = TILE + n_taps
    offsets = 2 * REACH + 1
    reach_devs = halos[-1][0]
    circle = slab + EDGE
    left_index = len(halos)

    barrier = pltpu.get_barrier_semaphore()
    pl.semaphore_signal(barrier, inc=1, device_id={"sub": 1 - sub}, device_id_type=MESH)

    def aper_partner(level):
        stride = 2**level
        side = lax.rem(aper // stride, 2)
        return aper + stride - 2 * stride * side, side

    for level in range(levels):
        pl.semaphore_signal(
            barrier, inc=1, device_id={"aper": aper_partner(level)[0]}, device_id_type=MESH
        )
    for dist in range(1, reach_devs + 1):
        @pl.when(rng + dist < n_rng)
        def _():
            pl.semaphore_signal(barrier, inc=1, device_id={"rng": rng + dist}, device_id_type=MESH)

        @pl.when(rng >= dist)
        def _():
            pl.semaphore_signal(barrier, inc=1, device_id={"rng": rng - dist}, device_id_type=MESH)

    own_copy = pltpu.make_async_copy(echoes, cells.at[:, :, pl.ds(EDGE, slab)], own_sem.at[0])
    own_copy.start()
    tables = ((phase_in, phase), (shift_in, shift), (ktaps_in, ktaps), (mshift_in, mshift),
              (kweights_in, kweights))
    loads = [
        pltpu.make_async_copy(src, dst, own_sem.at[1 + i]) for i, (src, dst) in enumerate(tables)
    ]
    for load in loads:
        load.start()
    if reach_devs >= n_rng - 1:
        rng_peers = n_rng - 1
    else:
        rng_peers = jnp.minimum(rng, reach_devs) + jnp.minimum(n_rng - 1 - rng, reach_devs)
    pl.semaphore_wait(barrier, 1 + levels + rng_peers)

    def right_copy(index):
        dist, start, count = halos[index]
        return pltpu.make_async_remote_copy(
            src_ref=echoes.at[:, :, pl.ds(start, count)],
            dst_ref=cells.at[:, :, pl.ds(EDGE + dist * slab + start, count)],
            send_sem=halo_send.at[index],
            recv_sem=halo_recv.at[index],
            device_id={"rng": rng - dist},
            device_id_type=MESH,
        )

    left_copy = pltpu.make_async_remote_copy(
        src_ref=echoes.at[:, :, pl.ds(slab - EDGE, EDGE)],
        dst_ref=cells.at[:, :, pl.ds(0, EDGE)],
        send_sem=halo_send.at[left_index],
        recv_sem=halo_recv.at[left_index],
        device_id={"rng": rng + 1},
        device_id_type=MESH,
    )
    for index, (dist, start, count) in enumerate(halos):
        @pl.when(rng >= dist)
        def _():
            right_copy(index).start()

        @pl.when(rng + dist >= n_rng)
        def _():
            first = EDGE + dist * slab + start
            cells[:, :, first : first + count] = jnp.zeros((2, local, count), BF16)

    @pl.when(rng + 1 < n_rng)
    def _():
        left_copy.start()

    @pl.when(rng == 0)
    def _():
        cells[:, :, 0:EDGE] = jnp.zeros((2, local, EDGE), BF16)

    def sub_copy(src, dst, index):
        return pltpu.make_async_remote_copy(
            src_ref=src,
            dst_ref=dst,
            send_sem=sub_send.at[index],
            recv_sem=sub_recv.at[index],
            device_id={"sub": 1 - sub},
            device_id_type=MESH,
        )

    phase_copy = sub_copy(phase_in, phases, 0)
    shift_copy = sub_copy(shift_in, shifts, 1)
    phase_copy.start()
    shift_copy.start()

    taps_row = jnp.concatenate(
        [chirp[...].astype(F32), jnp.zeros((2, window - n_taps), F32)], axis=1
    )
    for part in range(2):
        spread = jnp.broadcast_to(taps_row[part : part + 1, :], (TILE, window))
        filt[part * TILE : (part + 1) * TILE, :] = pltpu.roll(
            spread, 0, 1, stride=1, stride_axis=0
        ).astype(BF16)

    for load in loads:
        load.wait()

    beam_ids = lax.broadcasted_iota(jnp.int32, (beams, rows), 0)
    for level in range(levels):
        for child in range(2):
            tap = ktaps[level, child]
            real_w, imag_w = kweights[0, level, child], kweights[1, level, child]
            tap2 = jnp.concatenate([tap, tap], axis=1)
            upper_w = jnp.concatenate([real_w, imag_w], axis=1)
            lower_w = jnp.concatenate([-imag_w, real_w], axis=1)
            upper = jnp.zeros((beams, rows), F32)
            lower = jnp.zeros((beams, rows), F32)
            for t in range(tap.shape[0]):
                match = beam_ids == tap2[t : t + 1, :]
                upper = upper + jnp.where(match, upper_w[t : t + 1, :], 0.0)
                lower = lower + jnp.where(match, lower_w[t : t + 1, :], 0.0)
            kernels[level, child] = jnp.concatenate([upper, lower], axis=0).T.astype(BF16)
            row = mshift[level, child : child + 1, :]
            row2 = jnp.concatenate([row, row], axis=1) + REACH
            row_shift[level, child] = jnp.broadcast_to(row2, (rows, rows)).T

    phase_copy.wait()
    shift_copy.wait()

    def own_beams(own, got):
        stacked = jnp.concatenate([own, own, got, got], axis=0).T
        return jnp.where(sub == 0, stacked[:beams], stacked[beams:])

    angle = own_beams(phase[...], phases[...])
    lag = own_beams(shift[...], shifts[...])
    scale = 1.0 / math.sqrt(2 * local)
    cosine, sine = jnp.cos(angle) * scale, jnp.sin(angle) * scale
    is_real = lax.rem(lax.broadcasted_iota(jnp.int32, (beams, 4 * local), 1), 2 * local) < local
    upper = jnp.where(is_real, cosine, -sine)
    lower = jnp.where(is_real, sine, cosine)
    for index in range(offsets):
        match = lag == index - REACH
        select[index * rows : index * rows + beams, :] = jnp.where(match, upper, 0.0).astype(BF16)
        select[index * rows + beams : (index + 1) * rows, :] = jnp.where(
            match, lower, 0.0
        ).astype(BF16)

    own_copy.wait()

    def valid(first, columns):
        bins = lax.broadcasted_iota(jnp.int32, (8, columns), 1) + (first - EDGE) + rng * slab
        return ((bins >= 0) & (bins < n_rng * slab))[0:1]

    tiles = width // TILE
    order = list(range(1, tiles))
    order.insert(1, 0)

    def pulse_copy(tile):
        at = pl.ds(tile * TILE, TILE)
        return sub_copy(pulses.at[0, :, :, at], pulses.at[1, :, :, at], 2 + tile)

    def project(tile):
        first = tile * TILE
        pulse_copy(tile).wait_recv()
        block = pulses[:, :, :, first : first + TILE].reshape(4 * local, TILE)
        products[:, first : first + TILE] = jnp.dot(
            select[...], block, preferred_element_type=F32
        )

    arrived = 0
    for step, tile in enumerate(order):
        first = tile * TILE
        if step == 2:
            project(order[0])
            project(order[1])
        if tile == 0:
            @pl.when(rng > 0)
            def _():
                left_copy.wait_recv()
        while arrived < len(halos):
            dist, start, count = halos[arrived]
            if EDGE + dist * slab + start >= first + window:
                break

            @pl.when(rng + dist < n_rng)
            def _():
                right_copy(arrived).wait_recv()

            arrived += 1
        data = cells[:, :, first : first + window].reshape(2 * local, window)
        both = lax.dot_general(
            data, filt[...], (((1,), (1,)), ((), ())), preferred_element_type=F32
        )
        keep = valid(first, TILE)
        real = both[:local, :TILE] + both[local:, TILE:]
        imag = both[local:, :TILE] - both[:local, TILE:]
        pulses[0, 0, :, first : first + TILE] = jnp.where(keep, real, 0.0).astype(BF16)
        pulses[0, 1, :, first : first + TILE] = jnp.where(keep, imag, 0.0).astype(BF16)
        pulse_copy(tile).start()

    for tile in order[2:] if len(order) > 2 else order:
        project(tile)

    chunk = 16
    chunks = rows // chunk
    column = lax.broadcasted_iota(jnp.int32, (8, circle), 1)
    bins = jnp.where(column < slab + HALF, column, column - circle) + rng * slab
    keep_all = ((bins >= 0) & (bins < n_rng * slab))[0:1]
    is_next = lax.broadcasted_iota(jnp.int32, (8, EDGE), 1) < HALF

    def level_copy(level, piece):
        return pltpu.make_async_remote_copy(
            src_ref=image.at[level, pl.ds(piece * chunk, chunk)],
            dst_ref=sibling.at[level, pl.ds(piece * chunk, chunk)],
            send_sem=lev_send.at[level * chunks + piece],
            recv_sem=lev_recv.at[level * chunks + piece],
            device_id={"aper": aper_partner(level)[0]},
            device_id_type=MESH,
        )

    for piece in range(chunks):
        for half in range(2):
            at = piece * chunk + half * 8
            total = jnp.zeros((8, circle), F32)
            for index in range(offsets):
                here = index * rows + at
                margin = jnp.where(
                    is_next,
                    products[here : here + 8, EDGE + slab :],
                    products[here : here + 8, :EDGE],
                )
                part = jnp.concatenate(
                    [products[here : here + 8, EDGE : EDGE + slab], margin], axis=1
                )
                total = total + roll_left(part, index - REACH)
            products[at : at + 8, :circle] = jnp.where(keep_all, total, 0.0)
        image[0, piece * chunk : (piece + 1) * chunk, :] = products[
            piece * chunk : (piece + 1) * chunk, :circle
        ].astype(BF16)
        level_copy(0, piece).start()

    def moved(level, child_of, source):
        matrix = jnp.where(child_of == 0, kernels[level, 0], kernels[level, 1])
        by = jnp.where(child_of == 0, row_shift[level, 0], row_shift[level, 1])
        value = jnp.dot(matrix, source, preferred_element_type=F32)
        out_rows = []
        for first in range(0, rows, 8):
            part = value[first : first + 8]
            lanes = by[first : first + 8, 0:1]
            bit = 1
            while bit <= 2 * REACH:
                part = jnp.where((lanes & bit) != 0, roll_left(part, bit), part)
                bit *= 2
            out_rows.append(part)
        return out_rows

    for level in range(levels):
        side = aper_partner(level)[1]
        own = moved(level, side, image[level])
        for first in range(0, rows, 8):
            products[first : first + 8, :circle] = own[first // 8]
        for piece in range(chunks):
            level_copy(level, piece).wait_recv()
        other = moved(level, 1 - side, sibling[level])
        for piece in range(chunks):
            at = piece * chunk
            merged = jnp.concatenate(
                [
                    jnp.where(
                        keep_all,
                        roll_left(products[a : a + 8, :circle] + other[a // 8], -REACH),
                        0.0,
                    )
                    for a in (at, at + 8)
                ],
                axis=0,
            ).astype(BF16)
            if level < levels - 1:
                image[level + 1, at : at + chunk, :] = merged
                level_copy(level + 1, piece).start()
            else:
                out[at // beams, at % beams : at % beams + chunk, :] = merged[
                    :, :slab
                ]

    pl_levels = range(levels)
    for level in pl_levels:
        for piece in range(chunks):
            level_copy(level, piece).wait_send()
    for tile in order:
        pulse_copy(tile).wait_send()
    for index, (dist, _, _) in enumerate(halos):
        @pl.when(rng >= dist)
        def _():
            right_copy(index).wait_send()

    @pl.when(rng + 1 < n_rng)
    def _():
        left_copy.wait_send()


def shards(n_rng, n_aper, echoes, chirp, phase, shift, ktaps, mshift, kweights):
    local, slab = echoes.shape[1], echoes.shape[2]
    n_taps = chirp.shape[1]
    beams = ktaps.shape[3]
    rows = 2 * beams
    levels = n_aper.bit_length() - 1
    width = slab + 2 * EDGE
    halos = []
    at = 0
    while at < n_taps + EDGE:
        ends = ((at + EDGE) // TILE * TILE + EDGE, (at // slab + 1) * slab, n_taps + EDGE)
        end = min(e for e in ends if e > at)
        halos.append((at // slab + 1, at % slab, end - at))
        at = end
    halo = n_taps + EDGE
    offsets = 2 * REACH + 1
    pieces = levels * (rows // 16)
    vmem = pl.BlockSpec(memory_space=pltpu.VMEM)
    hbm = pl.BlockSpec(memory_space=pltpu.HBM)
    tables = (phase, shift, ktaps, mshift, kweights)
    return pl.pallas_call(
        functools.partial(image_kernel, n_rng, n_aper, levels, tuple(halos)),
        out_shape=jax.ShapeDtypeStruct((2, beams, slab), BF16),
        in_specs=[hbm, vmem] + [hbm] * 5,
        out_specs=vmem,
        scratch_shapes=[pltpu.VMEM(t.shape, t.dtype) for t in tables] + [
            pltpu.VMEM((2, local, EDGE + slab + halo), BF16),
            pltpu.VMEM((2 * TILE, TILE + n_taps), BF16),
            pltpu.VMEM(phase.shape, F32),
            pltpu.VMEM(shift.shape, jnp.int32),
            pltpu.VMEM((offsets * rows, 4 * local), BF16),
            pltpu.VMEM((2, 2, local, width), BF16),
            pltpu.VMEM((offsets * rows, width), F32),
            pltpu.VMEM((levels, rows, slab + EDGE), BF16),
            pltpu.VMEM((levels, rows, slab + EDGE), BF16),
            pltpu.VMEM((levels, 2, rows, rows), BF16),
            pltpu.VMEM((levels, 2, rows, rows), jnp.int32),
            pltpu.SemaphoreType.DMA((6,)),
            pltpu.SemaphoreType.DMA((len(halos) + 1,)),
            pltpu.SemaphoreType.DMA((len(halos) + 1,)),
            pltpu.SemaphoreType.DMA((2 + width // TILE,)),
            pltpu.SemaphoreType.DMA((2 + width // TILE,)),
            pltpu.SemaphoreType.DMA((pieces,)),
            pltpu.SemaphoreType.DMA((pieces,)),
        ],
        compiler_params=pltpu.CompilerParams(
            collective_id=0, has_side_effects=True, vmem_limit_bytes=64 * 2**20 - 2**17
        ),
    )(echoes, chirp, phase, shift, ktaps, mshift, kweights)


def solution(mesh):
    placed = (
        P(None, ("parts", "aper", "sub"), "rng"),
        P(),
        P(("parts", "aper", "sub"), None),
        P(("parts", "aper", "sub"), None),
        P(None, None, None, ("parts", "aper", "sub")),
        P(None, None, ("parts", "aper", "sub")),
        P(None, None, None, None, ("parts", "aper", "sub")),
    )
    return jax.shard_map(
        functools.partial(shards, mesh.shape["rng"], mesh.shape["aper"]),
        mesh=mesh,
        in_specs=placed,
        out_specs=P(None, ("parts", "aper", "sub"), "rng"),
        check_vma=False,
    )
```

```python
import functools
import math

import jax
import jax.numpy as jnp
from jax import lax
from jax.experimental import pallas as pl
from jax.experimental.pallas import tpu as pltpu
from jax.sharding import PartitionSpec as P

REACH = 8
EDGE = 128
HALF = EDGE // 2
TILE = 256
MESH = pl.DeviceIdType.MESH
F32 = jnp.float32
BF16 = jnp.bfloat16


def roll_left(value, by):
    width = value.shape[1]
    by = by % width
    return value if by == 0 else pltpu.roll(value, width - by, 1)


def image_kernel(
    n_rng, n_aper, levels, halos,
    echoes, chirp, phase_in, shift_in, ktaps_in, mshift_in, kweights_in,
    out,
    phase, shift, ktaps, mshift, kweights, cells, filt, phases, shifts, select, pulses, products, image, sibling, kernels, row_shift,
    own_sem, halo_send, halo_recv, sub_send, sub_recv, lev_send, lev_recv,
):
    rng = lax.axis_index("rng")
    aper = lax.axis_index("aper")
    sub = lax.axis_index("sub")
    local, slab = echoes.shape[1], echoes.shape[2]
    n_taps = chirp.shape[1]
    beams = out.shape[1]
    rows = 2 * beams
    width = slab + 2 * EDGE
    window = TILE + n_taps
    offsets = 2 * REACH + 1
    reach_devs = halos[-1][0]
    circle = slab + EDGE
    left_index = len(halos)

    barrier = pltpu.get_barrier_semaphore()
    pl.semaphore_signal(barrier, inc=1, device_id={"sub": 1 - sub}, device_id_type=MESH)

    def aper_partner(level):
        stride = 2**level
        side = lax.rem(aper // stride, 2)
        return aper + stride - 2 * stride * side, side

    for level in range(levels):
        pl.semaphore_signal(
            barrier, inc=1, device_id={"aper": aper_partner(level)[0]}, device_id_type=MESH
        )
    for dist in range(1, reach_devs + 1):
        @pl.when(rng + dist < n_rng)
        def _():
            pl.semaphore_signal(barrier, inc=1, device_id={"rng": rng + dist}, device_id_type=MESH)

        @pl.when(rng >= dist)
        def _():
            pl.semaphore_signal(barrier, inc=1, device_id={"rng": rng - dist}, device_id_type=MESH)

    own_copy = pltpu.make_async_copy(echoes, cells.at[:, :, pl.ds(EDGE, slab)], own_sem.at[0])
    own_copy.start()
    tables = ((phase_in, phase), (shift_in, shift), (ktaps_in, ktaps), (mshift_in, mshift),
              (kweights_in, kweights))
    loads = [
        pltpu.make_async_copy(src, dst, own_sem.at[1 + i]) for i, (src, dst) in enumerate(tables)
    ]
    for load in loads:
        load.start()
    if reach_devs >= n_rng - 1:
        rng_peers = n_rng - 1
    else:
        rng_peers = jnp.minimum(rng, reach_devs) + jnp.minimum(n_rng - 1 - rng, reach_devs)
    pl.semaphore_wait(barrier, 1 + levels + rng_peers)

    def right_copy(index):
        dist, start, count = halos[index]
        return pltpu.make_async_remote_copy(
            src_ref=echoes.at[:, :, pl.ds(start, count)],
            dst_ref=cells.at[:, :, pl.ds(EDGE + dist * slab + start, count)],
            send_sem=halo_send.at[index],
            recv_sem=halo_recv.at[index],
            device_id={"rng": rng - dist},
            device_id_type=MESH,
        )

    left_copy = pltpu.make_async_remote_copy(
        src_ref=echoes.at[:, :, pl.ds(slab - EDGE, EDGE)],
        dst_ref=cells.at[:, :, pl.ds(0, EDGE)],
        send_sem=halo_send.at[left_index],
        recv_sem=halo_recv.at[left_index],
        device_id={"rng": rng + 1},
        device_id_type=MESH,
    )
    for index, (dist, start, count) in enumerate(halos):
        @pl.when(rng >= dist)
        def _():
            right_copy(index).start()

        @pl.when(rng + dist >= n_rng)
        def _():
            first = EDGE + dist * slab + start
            cells[:, :, first : first + count] = jnp.zeros((2, local, count), BF16)

    @pl.when(rng + 1 < n_rng)
    def _():
        left_copy.start()

    @pl.when(rng == 0)
    def _():
        cells[:, :, 0:EDGE] = jnp.zeros((2, local, EDGE), BF16)

    def sub_copy(src, dst, index):
        return pltpu.make_async_remote_copy(
            src_ref=src,
            dst_ref=dst,
            send_sem=sub_send.at[index],
            recv_sem=sub_recv.at[index],
            device_id={"sub": 1 - sub},
            device_id_type=MESH,
        )

    phase_copy = sub_copy(phase_in, phases, 0)
    shift_copy = sub_copy(shift_in, shifts, 1)
    phase_copy.start()
    shift_copy.start()

    taps_row = jnp.concatenate(
        [chirp[...].astype(F32), jnp.zeros((2, window - n_taps), F32)], axis=1
    )
    for part in range(2):
        spread = jnp.broadcast_to(taps_row[part : part + 1, :], (TILE, window))
        filt[part * TILE : (part + 1) * TILE, :] = pltpu.roll(
            spread, 0, 1, stride=1, stride_axis=0
        ).astype(BF16)

    for load in loads:
        load.wait()

    phase_copy.wait()
    shift_copy.wait()

    def own_beams(own, got):
        stacked = jnp.concatenate([own, own, got, got], axis=0).T
        return jnp.where(sub == 0, stacked[:beams], stacked[beams:])

    angle = own_beams(phase[...], phases[...])
    lag = own_beams(shift[...], shifts[...])
    scale = 1.0 / math.sqrt(2 * local)
    cosine, sine = jnp.cos(angle) * scale, jnp.sin(angle) * scale
    is_real = lax.rem(lax.broadcasted_iota(jnp.int32, (beams, 4 * local), 1), 2 * local) < local
    upper = jnp.where(is_real, cosine, -sine)
    lower = jnp.where(is_real, sine, cosine)
    for index in range(offsets):
        match = lag == index - REACH
        select[index * rows : index * rows + beams, :] = jnp.where(match, upper, 0.0).astype(BF16)
        select[index * rows + beams : (index + 1) * rows, :] = jnp.where(
            match, lower, 0.0
        ).astype(BF16)

    own_copy.wait()

    def valid(first, columns):
        bins = lax.broadcasted_iota(jnp.int32, (8, columns), 1) + (first - EDGE) + rng * slab
        return ((bins >= 0) & (bins < n_rng * slab))[0:1]

    tiles = width // TILE
    order = list(range(1, tiles))
    order.insert(1, 0)

    def pulse_copy(tile):
        at = pl.ds(tile * TILE, TILE)
        return sub_copy(pulses.at[0, :, :, at], pulses.at[1, :, :, at], 2 + tile)

    arrived = 0
    for tile in order:
        first = tile * TILE
        if tile == 0:
            @pl.when(rng > 0)
            def _():
                left_copy.wait_recv()
        while arrived < len(halos):
            dist, start, count = halos[arrived]
            if EDGE + dist * slab + start >= first + window:
                break

            @pl.when(rng + dist < n_rng)
            def _():
                right_copy(arrived).wait_recv()

            arrived += 1
        data = cells[:, :, first : first + window].reshape(2 * local, window)
        both = lax.dot_general(
            data, filt[...], (((1,), (1,)), ((), ())), preferred_element_type=F32
        )
        keep = valid(first, TILE)
        real = both[:local, :TILE] + both[local:, TILE:]
        imag = both[local:, :TILE] - both[:local, TILE:]
        pulses[0, 0, :, first : first + TILE] = jnp.where(keep, real, 0.0).astype(BF16)
        pulses[0, 1, :, first : first + TILE] = jnp.where(keep, imag, 0.0).astype(BF16)
        pulse_copy(tile).start()

    for tile in order:
        first = tile * TILE
        pulse_copy(tile).wait_recv()
        block = pulses[:, :, :, first : first + TILE].reshape(4 * local, TILE)
        products[:, first : first + TILE] = jnp.dot(
            select[...], block, preferred_element_type=F32
        )

    chunk = 16
    chunks = rows // chunk
    column = lax.broadcasted_iota(jnp.int32, (8, circle), 1)
    bins = jnp.where(column < slab + HALF, column, column - circle) + rng * slab
    keep_all = ((bins >= 0) & (bins < n_rng * slab))[0:1]
    is_next = lax.broadcasted_iota(jnp.int32, (8, EDGE), 1) < HALF

    def level_copy(level, piece):
        return pltpu.make_async_remote_copy(
            src_ref=image.at[level, pl.ds(piece * chunk, chunk)],
            dst_ref=sibling.at[level, pl.ds(piece * chunk, chunk)],
            send_sem=lev_send.at[level * chunks + piece],
            recv_sem=lev_recv.at[level * chunks + piece],
            device_id={"aper": aper_partner(level)[0]},
            device_id_type=MESH,
        )

    for piece in range(chunks):
        for half in range(2):
            at = piece * chunk + half * 8
            total = jnp.zeros((8, circle), F32)
            for index in range(offsets):
                here = index * rows + at
                margin = jnp.where(
                    is_next,
                    products[here : here + 8, EDGE + slab :],
                    products[here : here + 8, :EDGE],
                )
                part = jnp.concatenate(
                    [products[here : here + 8, EDGE : EDGE + slab], margin], axis=1
                )
                total = total + roll_left(part, index - REACH)
            products[at : at + 8, :circle] = jnp.where(keep_all, total, 0.0)
        image[0, piece * chunk : (piece + 1) * chunk, :] = products[
            piece * chunk : (piece + 1) * chunk, :circle
        ].astype(BF16)
        level_copy(0, piece).start()

    beam_ids = lax.broadcasted_iota(jnp.int32, (beams, rows), 0)
    for level in range(levels):
        for child in range(2):
            tap = ktaps[level, child]
            real_w, imag_w = kweights[0, level, child], kweights[1, level, child]
            tap2 = jnp.concatenate([tap, tap], axis=1)
            upper_w = jnp.concatenate([real_w, imag_w], axis=1)
            lower_w = jnp.concatenate([-imag_w, real_w], axis=1)
            upper = jnp.zeros((beams, rows), F32)
            lower = jnp.zeros((beams, rows), F32)
            for t in range(tap.shape[0]):
                match = beam_ids == tap2[t : t + 1, :]
                upper = upper + jnp.where(match, upper_w[t : t + 1, :], 0.0)
                lower = lower + jnp.where(match, lower_w[t : t + 1, :], 0.0)
            kernels[level, child] = jnp.concatenate([upper, lower], axis=0).T.astype(BF16)
            row = mshift[level, child : child + 1, :]
            row2 = jnp.concatenate([row, row], axis=1) + REACH
            row_shift[level, child] = jnp.broadcast_to(row2, (rows, rows)).T

    def moved(level, child_of, source):
        matrix = jnp.where(child_of == 0, kernels[level, 0], kernels[level, 1])
        by = jnp.where(child_of == 0, row_shift[level, 0], row_shift[level, 1])
        value = jnp.dot(matrix, source, preferred_element_type=F32)
        out_rows = []
        for first in range(0, rows, 8):
            part = value[first : first + 8]
            lanes = by[first : first + 8, 0:1]
            bit = 1
            while bit <= 2 * REACH:
                part = jnp.where((lanes & bit) != 0, roll_left(part, bit), part)
                bit *= 2
            out_rows.append(part)
        return out_rows

    for level in range(levels):
        side = aper_partner(level)[1]
        own = moved(level, side, image[level])
        for first in range(0, rows, 8):
            products[first : first + 8, :circle] = own[first // 8]
        for piece in range(chunks):
            level_copy(level, piece).wait_recv()
        other = moved(level, 1 - side, sibling[level])
        for piece in range(chunks):
            at = piece * chunk
            merged = jnp.concatenate(
                [
                    jnp.where(
                        keep_all,
                        roll_left(products[a : a + 8, :circle] + other[a // 8], -REACH),
                        0.0,
                    )
                    for a in (at, at + 8)
                ],
                axis=0,
            ).astype(BF16)
            if level < levels - 1:
                image[level + 1, at : at + chunk, :] = merged
                level_copy(level + 1, piece).start()
            else:
                out[at // beams, at % beams : at % beams + chunk, :] = merged[
                    :, :slab
                ]

    pl_levels = range(levels)
    for level in pl_levels:
        for piece in range(chunks):
            level_copy(level, piece).wait_send()
    for tile in order:
        pulse_copy(tile).wait_send()
    for index, (dist, _, _) in enumerate(halos):
        @pl.when(rng >= dist)
        def _():
            right_copy(index).wait_send()

    @pl.when(rng + 1 < n_rng)
    def _():
        left_copy.wait_send()


def shards(n_rng, n_aper, echoes, chirp, phase, shift, ktaps, mshift, kweights):
    local, slab = echoes.shape[1], echoes.shape[2]
    n_taps = chirp.shape[1]
    beams = ktaps.shape[3]
    rows = 2 * beams
    levels = n_aper.bit_length() - 1
    width = slab + 2 * EDGE
    halos = []
    at = 0
    while at < n_taps + EDGE:
        ends = ((at + EDGE) // TILE * TILE + EDGE, (at // slab + 1) * slab, n_taps + EDGE)
        end = min(e for e in ends if e > at)
        halos.append((at // slab + 1, at % slab, end - at))
        at = end
    halo = n_taps + EDGE
    offsets = 2 * REACH + 1
    pieces = levels * (rows // 16)
    vmem = pl.BlockSpec(memory_space=pltpu.VMEM)
    hbm = pl.BlockSpec(memory_space=pltpu.HBM)
    tables = (phase, shift, ktaps, mshift, kweights)
    return pl.pallas_call(
        functools.partial(image_kernel, n_rng, n_aper, levels, tuple(halos)),
        out_shape=jax.ShapeDtypeStruct((2, beams, slab), BF16),
        in_specs=[hbm, vmem] + [hbm] * 5,
        out_specs=vmem,
        scratch_shapes=[pltpu.VMEM(t.shape, t.dtype) for t in tables] + [
            pltpu.VMEM((2, local, EDGE + slab + halo), BF16),
            pltpu.VMEM((2 * TILE, TILE + n_taps), BF16),
            pltpu.VMEM(phase.shape, F32),
            pltpu.VMEM(shift.shape, jnp.int32),
            pltpu.VMEM((offsets * rows, 4 * local), BF16),
            pltpu.VMEM((2, 2, local, width), BF16),
            pltpu.VMEM((offsets * rows, width), F32),
            pltpu.VMEM((levels, rows, slab + EDGE), BF16),
            pltpu.VMEM((levels, rows, slab + EDGE), BF16),
            pltpu.VMEM((levels, 2, rows, rows), BF16),
            pltpu.VMEM((levels, 2, rows, rows), jnp.int32),
            pltpu.SemaphoreType.DMA((6,)),
            pltpu.SemaphoreType.DMA((len(halos) + 1,)),
            pltpu.SemaphoreType.DMA((len(halos) + 1,)),
            pltpu.SemaphoreType.DMA((2 + width // TILE,)),
            pltpu.SemaphoreType.DMA((2 + width // TILE,)),
            pltpu.SemaphoreType.DMA((pieces,)),
            pltpu.SemaphoreType.DMA((pieces,)),
        ],
        compiler_params=pltpu.CompilerParams(
            collective_id=0, has_side_effects=True, vmem_limit_bytes=64 * 2**20 - 2**17
        ),
    )(echoes, chirp, phase, shift, ktaps, mshift, kweights)


def solution(mesh):
    placed = (
        P(None, ("parts", "aper", "sub"), "rng"),
        P(),
        P(("parts", "aper", "sub"), None),
        P(("parts", "aper", "sub"), None),
        P(None, None, None, ("parts", "aper", "sub")),
        P(None, None, ("parts", "aper", "sub")),
        P(None, None, None, None, ("parts", "aper", "sub")),
    )
    return jax.shard_map(
        functools.partial(shards, mesh.shape["rng"], mesh.shape["aper"]),
        mesh=mesh,
        in_specs=placed,
        out_specs=P(None, ("parts", "aper", "sub"), "rng"),
        check_vma=False,
    )
```
